256 devices in a mesh: inner: 16 (over z_hi, x, core), outer: 16 (over z_lo, y).
Axes of the slice: x: 4, y: 4, z: 8 (z_hi: 2, z_lo: 4; z = z_hi * 4 + z_lo), core: 2. Of those that a mesh axis runs over, the one named last changes fastest.
Arguments:
- queries: bfloat16 [98304, 1024], P(('inner', 'outer')), may hold values from -10 to 10
- key_rows: bfloat16 [98304, 1024], P(('inner', 'outer')), may hold values from -10 to 10
- value_rows: bfloat16 [98304, 1024], P(('inner', 'outer')), may hold values from -6 to 6
- cotangent: bfloat16 [98304, 1024], P(('inner', 'outer')), may hold values from -6 to 6
- page_mask: int32 [768, 3, 3], replicated, may hold values from 0 to 1, as said below
Outputs:
- grad_query: bfloat16 [98304, 1024], P(('inner', 'outer'))
- grad_key: bfloat16 [98304, 1024], P(('inner', 'outer'))
- grad_value: bfloat16 [98304, 1024], P(('inner', 'outer'))
The draws below stay inside these ranges and needn't reach their ends.
Inputs may be any that keep to these rules, and one draw needn't show every extreme that they name: For query page p in block b = p // 3: page_mask[p, 0, p % 3] = 1 and page_mask[p, 0, j] = 0 for j > p % 3; page_mask[p, 1, :] is all zero when b % 16 == 0, and page_mask[p, 2, :] when b < 16.
All inputs are finite; a program needn't handle non-finite values.
Results may differ from the reference program's by a relative error of at most 0.0051.
Values may be sent and summed in bfloat16 or wider, within the bound.
No kernel may reach another device: no remote copies, remote signals or barrier semaphores. Data moves between devices by JAX's collectives and lax.ppermute only.
A program may use at most 192 MiB of HBM per device.

```python
import math
import jax
import jax.numpy as jnp
from jax import lax

HEADS = 8
HEAD_DIM = 128
PAGE = 128
TOK_DEV = 384
PG = 3
HD = 1024
TOKENS = 98304
PAGES = 768
N_INNER = 16
N_OUTER = 16


def draw_queries(key, part):
    key = jax.random.fold_in(key, 7)
    drawn = jnp.clip(jax.random.normal(key, (TOKENS, HD)), -6.0, 6.0)
    return drawn.astype(jnp.bfloat16)


def draw_key_rows(key, part):
    key = jax.random.fold_in(key, 8)
    drawn = jnp.clip(jax.random.normal(key, (TOKENS, HD)), -6.0, 6.0)
    return drawn.astype(jnp.bfloat16)


def draw_page_mask(key, part):
    key = jax.random.fold_in(key, 9)
    block_count = PAGES // PG
    levels = jax.random.randint(jax.random.fold_in(key, 1), (block_count, 1, 1, 1), 0, 4)
    coin_flips = jax.random.randint(jax.random.fold_in(key, 2), (block_count, PG, 3, PG), 0, 8)
    picked = coin_flips < jnp.left_shift(jnp.int32(1), levels)
    block_ids = jnp.arange(block_count, dtype=jnp.int32)[:, None, None, None]
    outer_ids = block_ids % N_OUTER
    inner_ids = block_ids // N_OUTER
    query_page = jnp.arange(PG, dtype=jnp.int32)[None, :, None, None]
    source = jnp.arange(3, dtype=jnp.int32)[None, None, :, None]
    key_page = jnp.arange(PG, dtype=jnp.int32)[None, None, None, :]
    own_part = jnp.logical_or(key_page == query_page, jnp.logical_and(picked, key_page < query_page))
    near_part = jnp.logical_and(picked, outer_ids > 0)
    far_part = jnp.logical_and(picked, inner_ids > 0)
    chosen = jnp.where(source == 0, own_part, jnp.where(source == 1, near_part, far_part))
    return chosen.astype(jnp.int32).reshape(PAGES, 3, PG)


def block_levels(stream_key, extent, cuts, smallest, high):
    level = 1.0
    for dim, parts in cuts:
        heights = jax.random.uniform(jax.random.fold_in(jax.random.fold_in(stream_key, 6), dim), (parts,), jnp.float32, smallest / len(cuts), high / len(cuts))
        level = level * jnp.repeat(jnp.exp(heights), extent[dim] // parts).reshape((-1,) + (1,) * (len(extent) - 1 - dim))
    return level


def centred(own_key, shape, deviation, limit, cuts=(), held_as=jnp.bfloat16):
    loudness = block_levels(own_key, shape, cuts, -0.22, 0.18) if cuts else 1.0
    values = jax.random.normal(own_key, shape, jnp.float32) * deviation * loudness
    return jnp.minimum(jnp.maximum(values, -limit), limit).astype(held_as)


def setup_inputs(seed: int = 0) -> dict:
    streams_of = jax.random.split(jax.random.key(seed), 6)
    queries = draw_queries(jax.random.fold_in(streams_of[5], 71), 0)
    key_rows = draw_key_rows(jax.random.fold_in(streams_of[5], 71), 0)
    value_rows = centred(streams_of[2], (TOKENS, HD), 1.0, 6.0, ((0, 256),))
    cotangent = centred(streams_of[3], (TOKENS, HD), 1.0, 6.0, ((0, 256),))
    page_mask = draw_page_mask(jax.random.fold_in(streams_of[5], 71), 0)
    return {"queries": queries, "key_rows": key_rows, "value_rows": value_rows, "cotangent": cotangent, "page_mask": page_mask}


def split_heads(matrix):
    return matrix.reshape(matrix.shape[0], HEADS, HEAD_DIM).astype(jnp.float32)

def pair_parts(queries, cotangent, key_rows, value_rows):
    scaling = 1.0 / math.sqrt(HEAD_DIM)
    scores = jnp.einsum('thd,shd->hts', split_heads(queries), split_heads(key_rows)) * scaling
    pushes = jnp.einsum('thd,shd->hts', split_heads(cotangent), split_heads(value_rows))
    return (scores, pushes)

def pair_grads(queries, cotangent, key_rows, value_rows, allowed, log_total, correction, for_queries):
    scaling = 1.0 / math.sqrt(HEAD_DIM)
    scores, pushes = pair_parts(queries, cotangent, key_rows, value_rows)
    weighting = jnp.where(allowed[None], jnp.exp(scores - log_total[:, :, None]), 0.0)
    dscore = weighting * (pushes - correction[:, :, None])
    dscore_low = lax.optimization_barrier(dscore.astype(jnp.bfloat16)).astype(jnp.float32)
    if for_queries:
        grad_q = jnp.einsum('hts,shd->thd', dscore_low, split_heads(key_rows))
        return grad_q.reshape(queries.shape[0], HD) * scaling
    weight_low = lax.optimization_barrier(weighting.astype(jnp.bfloat16)).astype(jnp.float32)
    grad_v = jnp.einsum('hts,thd->shd', weight_low, split_heads(cotangent)).reshape(key_rows.shape[0], HD)
    grad_k = jnp.einsum('hts,thd->shd', dscore_low, split_heads(queries)).reshape(key_rows.shape[0], HD) * scaling
    return (grad_k, grad_v)

def reference(queries, key_rows, value_rows, cotangent, page_mask):
    block_count = N_INNER * N_OUTER

    def rows_of(array, block_at):
        first_row = (jnp.clip(block_at, 0, block_count - 1) * TOK_DEV).astype(jnp.int32)
        return lax.dynamic_slice_in_dim(array, first_row, TOK_DEV, 0)

    def mask_of(block_at, source):
        first_row = (jnp.clip(block_at, 0, block_count - 1) * PG).astype(jnp.int32)
        picked = lax.dynamic_slice_in_dim(page_mask, first_row, PG, 0)[:, source, :]
        expanded = jnp.broadcast_to(picked[:, None, :, None] > 0, (PG, PAGE, PG, PAGE)).reshape(TOK_DEV, TOK_DEV)
        if source == 0:
            row_ids = lax.broadcasted_iota(jnp.int32, (TOK_DEV, TOK_DEV), 0)
            col_ids = lax.broadcasted_iota(jnp.int32, (TOK_DEV, TOK_DEV), 1)
            expanded = jnp.logical_and(expanded, col_ids <= row_ids)
        inside = jnp.logical_and(block_at >= 0, block_at < block_count)
        return jnp.logical_and(expanded, inside)

    def statistics(block_at):
        partners = (block_at, block_at - 1, block_at - N_OUTER)
        key_all = jnp.concatenate([rows_of(key_rows, partner) for partner in partners], axis=0)
        value_all = jnp.concatenate([rows_of(value_rows, partner) for partner in partners], axis=0)
        allowed = jnp.concatenate([mask_of(block_at, source) for source in range(3)], axis=1)
        scores, pushes = pair_parts(rows_of(queries, block_at), rows_of(cotangent, block_at), key_all, value_all)
        log_total = jax.nn.logsumexp(jnp.where(allowed[None], scores, -jnp.inf), axis=2)
        weighting = jnp.where(allowed[None], jnp.exp(scores - log_total[:, :, None]), 0.0)
        return (log_total, lax.optimization_barrier(jnp.sum(weighting * pushes, axis=2)))
    block_ids = jnp.arange(block_count, dtype=jnp.int32)
    log_totals, corrections = lax.map(statistics, block_ids)

    def gradients(block_at):
        query_here = rows_of(queries, block_at)
        cotangent_here = rows_of(cotangent, block_at)
        key_here = rows_of(key_rows, block_at)
        value_here = rows_of(value_rows, block_at)
        grad_q = jnp.zeros((TOK_DEV, HD), jnp.float32)
        for source, partner in ((0, block_at), (1, block_at - 1), (2, block_at - N_OUTER)):
            grad_q = grad_q + pair_grads(query_here, cotangent_here, rows_of(key_rows, partner), rows_of(value_rows, partner), mask_of(block_at, source), log_totals[block_at], corrections[block_at], True)
        grad_k = jnp.zeros((TOK_DEV, HD), jnp.float32)
        grad_v = jnp.zeros((TOK_DEV, HD), jnp.float32)
        for source, partner in ((0, block_at), (1, block_at + 1), (2, block_at + N_OUTER)):
            clipped = jnp.clip(partner, 0, block_count - 1)
            part_k, part_v = pair_grads(rows_of(queries, partner), rows_of(cotangent, partner), key_here, value_here, mask_of(partner, source), log_totals[clipped], corrections[clipped], False)
            grad_k = grad_k + part_k
            grad_v = grad_v + part_v
        return (grad_q.astype(jnp.bfloat16), grad_k.astype(jnp.bfloat16), grad_v.astype(jnp.bfloat16))
    grad_q, grad_k, grad_v = lax.map(gradients, block_ids)
    return (grad_q.reshape(TOKENS, HD), grad_k.reshape(TOKENS, HD), grad_v.reshape(TOKENS, HD))
```

```python
import functools
import math

import jax
import jax.numpy as jnp
from jax import lax
from jax.experimental import pallas as pl
from jax.experimental.pallas import tpu as pltpu
from jax.sharding import PartitionSpec as P

HEADS = 8
D = 128
PAGE = 128
PG = 3
TOK = PG * PAGE
AXES = ("inner", "outer")
MASKED = -1e30
SCALE = 1.0 / math.sqrt(D)
SCALE2 = SCALE * math.log2(math.e)
GROUPS = ((0, 4), (4, 4))
NT = (((1,), (1,)), ((), ()))
NN = (((1,), (0,)), ((), ()))
TN = (((0,), (0,)), ((), ()))


def dot(a, b, dims):
    return lax.dot_general(a, b, dims, preferred_element_type=jnp.float32)


def causal_bias():
    key_at = lax.broadcasted_iota(jnp.int32, (PAGE, PAGE), 0)
    query_at = lax.broadcasted_iota(jnp.int32, (PAGE, PAGE), 1)
    return jnp.where(key_at <= query_at, 0.0, MASKED).astype(jnp.float32)


def strips(keys, values, queries, cotangent, bias, own, causal):
    for j in range(PG):
        lo = j * PAGE if own else 0
        rows = slice(j * PAGE, (j + 1) * PAGE)
        scores = dot(keys[rows], queries[lo:], NT) * SCALE2 + bias[j : j + 1, lo:]
        if own:
            first = scores[:, :PAGE] + causal
            scores = first if j == PG - 1 else jnp.concatenate((first, scores[:, PAGE:]), axis=1)
        pushes = dot(values[rows], cotangent[lo:], NT)
        yield j, lo, scores, pushes


def stats_kernel(count, q, do, k, v, nk, nv, fk, fv, bias, out):
    h = pl.program_id(0)
    queries, cotangent = q[...], do[...]
    biases = bias[...]
    causal = causal_bias()
    parts = []
    for src, (keys, values) in enumerate(((k, v), (nk, nv), (fk, fv))):
        parts += list(
            strips(
                keys[...], values[...], queries, cotangent,
                biases[3 * src : 3 * src + 3], src == 0, causal,
            )
        )
    tops, sums, moments = [], [], []
    for i in range(PG):
        cols = slice(i * PAGE, (i + 1) * PAGE)
        here = [
            (s[:, i * PAGE - lo : (i + 1) * PAGE - lo], p[:, i * PAGE - lo : (i + 1) * PAGE - lo])
            for j, lo, s, p in parts
            if lo <= i * PAGE
        ]
        top = functools.reduce(jnp.maximum, [s for s, _ in here])
        top = jnp.max(top, axis=0, keepdims=True)
        mass, moment = 0.0, 0.0
        for s, p in here:
            e = jnp.exp2(s - top)
            mass = mass + e
            moment = moment + e * p
        mass = jnp.sum(mass, axis=0, keepdims=True)
        moment = jnp.sum(moment, axis=0, keepdims=True)
        rows = lax.broadcasted_iota(jnp.int32, (2 * count, PAGE), 0)
        held = jnp.where(rows == count + h, moment / mass, out[:, cols])
        out[:, cols] = jnp.where(rows == h, top + jnp.log2(mass), held)


def row_of(stats, at):
    rows = lax.broadcasted_iota(jnp.int32, stats.shape, 0)
    return jnp.sum(jnp.where(rows == at, stats, 0.0), axis=0, keepdims=True)


def weights(scores, pushes, total, correction):
    prob = jnp.exp2(scores - total)
    dscore = prob * (pushes - correction)
    return prob.astype(jnp.bfloat16), dscore.astype(jnp.bfloat16)


def query_kernel(count, q, do, k, v, nk, nv, fk, fv, bias, stats, *rest):
    dq_out, dk_out, dv_out = rest[-3:]
    h = pl.program_id(0)
    queries, cotangent = q[...], do[...]
    biases = bias[...]
    total, correction = row_of(stats[...], h), row_of(stats[...], count + h)
    causal = causal_bias()
    grad_q = jnp.zeros((TOK, D), jnp.float32)
    for src, (keys, values) in enumerate(((k, v), (nk, nv), (fk, fv))):
        own = src == 0
        parts = []
        for j, lo, s, p in strips(
            keys[...], values[...], queries, cotangent, biases[3 * src : 3 * src + 3], own, causal
        ):
            prob, dscore = weights(s, p, total[:, lo:], correction[:, lo:])
            if own:
                rows = slice(j * PAGE, (j + 1) * PAGE)
                dv_out[rows] = dot(prob, cotangent[lo:], NN)
                dk_out[rows] = dot(dscore, queries[lo:], NN)
            if lo:
                dscore = jnp.concatenate((jnp.zeros((PAGE, lo), dscore.dtype), dscore), axis=1)
            parts.append(dscore)
        grad_q = grad_q + dot(jnp.concatenate(parts, axis=0), keys[...], TN)
    dq_out[...] = (grad_q * SCALE).astype(dq_out.dtype)


def key_kernel(count, k, v, own_dk, own_dv, nq, ndo, nstats, fq, fdo, fstats, bias, *rest):
    dk_out, dv_out = rest[-2:]
    h = pl.program_id(0)
    keys, values = k[...], v[...]
    biases = bias[...]
    lines = [
        (row_of(st[...], h), row_of(st[...], count + h)) for st in (nstats, fstats)
    ]
    for j in range(PG):
        rows = slice(j * PAGE, (j + 1) * PAGE)
        grad_k, grad_v = own_dk[rows], own_dv[rows]
        for src, (q, do) in enumerate(((nq, ndo), (fq, fdo))):
            queries, cotangent = q[...], do[...]
            at = 9 + 3 * src + j
            s = dot(keys[rows], queries, NT) * SCALE2 + biases[at : at + 1]
            p = dot(values[rows], cotangent, NT)
            prob, dscore = weights(s, p, *lines[src])
            grad_v = grad_v + dot(prob, cotangent, NN)
            grad_k = grad_k + dot(dscore, queries, NN)
        dk_out[rows] = (grad_k * SCALE).astype(dk_out.dtype)
        dv_out[rows] = grad_v.astype(dv_out.dtype)


def column(offset):
    return pl.BlockSpec((TOK, D), lambda h: (0, h + offset))


def whole(shape):
    return pl.BlockSpec(shape, lambda h: (0, 0))


def call(kernel, name, count, ins, outs, carried, pairs, dots):
    arrays = [a for a, _ in ins]
    in_specs = [s for _, s in ins]
    aliases = {}
    for at, array in enumerate(carried):
        aliases[len(arrays)] = at
        arrays.append(array)
        in_specs.append(pl.BlockSpec(memory_space=pl.ANY))
    return pl.pallas_call(
        functools.partial(kernel, count),
        name=name,
        grid=(count,),
        in_specs=in_specs,
        out_specs=[s for _, s in outs],
        out_shape=[s for s, _ in outs],
        input_output_aliases=aliases,
        compiler_params=pltpu.CompilerParams(
            dimension_semantics=("arbitrary",), vmem_limit_bytes=48 * 1024 * 1024
        ),
        cost_estimate=pl.CostEstimate(
            flops=2 * dots * count * TOK * TOK * D,
            bytes_accessed=len(ins) * count * TOK * D * 2,
            transcendentals=pairs * count * TOK * TOK,
        ),
    )(*arrays)


def biases_of(page_mask, block_at, block_count):
    flat = page_mask.reshape(block_count, PG, 3, PG)

    def picked(at, source):
        part = lax.dynamic_slice(
            flat, (jnp.minimum(at, block_count - 1), 0, source, 0), (1, PG, 1, PG)
        )
        inside = at < block_count
        part = jnp.where(inside, part.reshape(PG, PG).T, 0)
        return jnp.where(part > 0, 0.0, MASKED).astype(jnp.float32)

    rows = [picked(block_at, source) for source in range(3)]
    rows += [picked(block_at + 1, 1), picked(block_at + lax.axis_size("outer"), 2)]
    rows = jnp.concatenate(rows + [jnp.zeros((1, PG), jnp.float32)], axis=0)
    return jnp.broadcast_to(rows[:, :, None], (16, PG, PAGE)).reshape(16, TOK)


def body(queries, key_rows, value_rows, cotangent, page_mask):
    n_inner, n_outer = lax.axis_size("inner"), lax.axis_size("outer")
    block_at = lax.axis_index("inner") * n_outer + lax.axis_index("outer")
    near = [
        (i * n_outer + o, i * n_outer + o + 1) for i in range(n_inner) for o in range(n_outer - 1)
    ]
    far = [
        (i * n_outer + o, (i + 1) * n_outer + o) for i in range(n_inner - 1) for o in range(n_outer)
    ]
    near_back, far_back = [(b, a) for a, b in near], [(b, a) for a, b in far]

    def send(array, pairs):
        return lax.ppermute(array, AXES, pairs)

    moved = []
    for first, count in GROUPS:
        cols = slice(first * D, (first + count) * D)
        key_value = jnp.concatenate((key_rows[:, cols], value_rows[:, cols]), axis=1)
        query_cot = jnp.concatenate((queries[:, cols], cotangent[:, cols]), axis=1)
        moved.append(
            (
                send(key_value, near),
                send(query_cot, near_back),
                send(key_value, far),
                send(query_cot, far_back),
            )
        )
    bias = biases_of(page_mask, block_at, n_inner * n_outer)

    out = jax.ShapeDtypeStruct((TOK, HEADS * D), jnp.bfloat16)
    grad_q, grad_k, grad_v = None, None, None
    for (first, count), (near_kv, near_qc, far_kv, far_qc) in zip(GROUPS, moved):
        local = column(first)
        query_side = [
            (queries, local),
            (cotangent, local),
            (key_rows, local),
            (value_rows, local),
            (near_kv, column(0)),
            (near_kv, column(count)),
            (far_kv, column(0)),
            (far_kv, column(count)),
            (bias, whole((16, TOK))),
        ]
        stat_block = whole((2 * count, TOK))
        stat_shape = jax.ShapeDtypeStruct((2 * count, TOK), jnp.float32)
        (stats,) = call(
            stats_kernel, "stats", count, query_side, [(stat_shape, stat_block)], [], 3, 6
        )
        near_stats = send(stats, near_back)
        far_stats = send(stats, far_back)
        part = jax.ShapeDtypeStruct((TOK, count * D), jnp.float32)
        grad_q, own_dk, own_dv = call(
            query_kernel, "query_side", count,
            query_side + [(stats, stat_block)],
            [(out, local), (part, column(0)), (part, column(0))],
            [] if grad_q is None else [grad_q], 3, 11,
        )
        grad_k, grad_v = call(
            key_kernel, "key_side", count,
            [
                (key_rows, local),
                (value_rows, local),
                (own_dk, column(0)),
                (own_dv, column(0)),
                (near_qc, column(0)),
                (near_qc, column(count)),
                (near_stats, stat_block),
                (far_qc, column(0)),
                (far_qc, column(count)),
                (far_stats, stat_block),
                (bias, whole((16, TOK))),
            ],
            [(out, local), (out, local)],
            [] if grad_k is None else [grad_k, grad_v], 2, 8,
        )
    return (grad_q, grad_k, grad_v)


def solution(mesh):
    split = P(AXES, None)
    return jax.shard_map(
        body, mesh=mesh, in_specs=(split, split, split, split, P()),
        out_specs=(split, split, split), check_vma=False,
    )
```

```python
import functools
import math

import jax
import jax.numpy as jnp
from jax import lax
from jax.experimental import pallas as pl
from jax.experimental.pallas import tpu as pltpu
from jax.sharding import PartitionSpec as P

HEADS = 8
D = 128
PAGE = 128
PG = 3
TOK = PG * PAGE
AXES = ("inner", "outer")
MASKED = -1e30
SCALE = 1.0 / math.sqrt(D)
SCALE2 = SCALE * math.log2(math.e)
GROUPS = ((0, 4), (4, 4))
NT = (((1,), (1,)), ((), ()))
NN = (((1,), (0,)), ((), ()))
TN = (((0,), (0,)), ((), ()))


def dot(a, b, dims):
    return lax.dot_general(a, b, dims, preferred_element_type=jnp.float32)


def query_head(queries, cotangent, sources, biases):
    key_at = lax.broadcasted_iota(jnp.int32, (PAGE, PAGE), 0)
    causal = key_at <= lax.broadcasted_iota(jnp.int32, (PAGE, PAGE), 1)
    pages, tops, masses, moments = [], [], [], []
    for src, (keys, values) in enumerate(sources):
        scores, pushes = dot(keys, queries, NT), dot(values, cotangent, NT)
        for j in range(PG):
            lo = j * PAGE if src == 0 else 0
            rows = slice(j * PAGE, (j + 1) * PAGE)
            s, p = scores[rows, lo:], pushes[rows, lo:]
            if src == 0:
                diagonal = jnp.where(causal, s[:, :PAGE], MASKED)
                s = diagonal if j == PG - 1 else jnp.concatenate((diagonal, s[:, PAGE:]), axis=1)
            top = jnp.max(s, axis=0, keepdims=True)
            e = jnp.exp2((s - top) * SCALE2)
            mass = jnp.sum(e, axis=0, keepdims=True)
            moment = jnp.sum(e * p, axis=0, keepdims=True)
            top = top * SCALE2 + biases[3 * src + j : 3 * src + j + 1, lo:]
            if lo:
                zeros = jnp.zeros((1, lo), jnp.float32)
                top = jnp.concatenate((zeros + MASKED, top), axis=1)
                mass = jnp.concatenate((zeros, mass), axis=1)
                moment = jnp.concatenate((zeros, moment), axis=1)
            pages.append((e, p))
            tops.append(top)
            masses.append(mass)
            moments.append(moment)
    highest = functools.reduce(jnp.maximum, tops)
    factors = [jnp.exp2(top - highest) for top in tops]
    mass = functools.reduce(jnp.add, [f * m for f, m in zip(factors, masses)])
    moment = functools.reduce(jnp.add, [f * m for f, m in zip(factors, moments)])
    scale = 1.0 / mass
    correction = moment * scale
    grad_q = 0.0
    own = None
    for src, (keys, values) in enumerate(sources):
        probs, dscores = [], []
        for j in range(PG):
            lo = j * PAGE if src == 0 else 0
            e, p = pages[3 * src + j]
            prob = e * (factors[3 * src + j] * scale)[:, lo:]
            dscore = (prob * (p - correction[:, lo:])).astype(jnp.bfloat16)
            prob = prob.astype(jnp.bfloat16)
            if lo:
                zeros = jnp.zeros((PAGE, lo), jnp.bfloat16)
                dscore = jnp.concatenate((zeros, dscore), axis=1)
                prob = jnp.concatenate((zeros, prob), axis=1)
            dscores.append(dscore)
            probs.append(prob)
        dscore = jnp.concatenate(dscores, axis=0)
        if src == 0:
            own = (dot(dscore, queries, NN), dot(jnp.concatenate(probs, axis=0), cotangent, NN))
        grad_q = grad_q + dot(keys, dscore, TN)
    return highest + jnp.log2(mass), correction, (grad_q * SCALE).T, own


def pick(flag, usual, other, cols):
    return jnp.where(flag, other[:, cols], usual[:, cols])


def load(arrays, first, count, held, sems):
    cols = pl.ds(first * D, count * D)
    copies = [
        pltpu.make_async_copy(array.at[:, cols], held.at[n], sems.at[n])
        for n, array in enumerate(arrays)
    ]
    for copy in copies:
        copy.start()
    for copy in copies:
        copy.wait()
    return [held.at[n] for n in range(len(arrays))]


def query_kernel(first, count, flags, q, do, k, v, near, far, wrapped, bias, *rest):
    dq_out, stats, dk_out, dv_out, held, sems = rest[-6:]
    q, do, k, v = load((q, do, k, v), first, count, held, sems)
    biases = bias[...]
    totals, corrections = [], []
    for h in range(count):
        cols, second = slice(h * D, (h + 1) * D), slice((count + h) * D, (count + h + 1) * D)
        if wrapped is None:
            far_key, far_value = far[:, cols], far[:, second]
        else:
            use = flags[0] > 0
            far_key, far_value = pick(use, far, wrapped, cols), pick(use, far, wrapped, second)
        sources = ((k[:, cols], v[:, cols]), (near[:, cols], near[:, second]), (far_key, far_value))
        total, correction, grad_q, own = query_head(q[:, cols], do[:, cols], sources, biases)
        totals.append(total)
        corrections.append(correction)
        dq_out[:, cols] = grad_q.astype(dq_out.dtype)
        dk_out[:, cols], dv_out[:, cols] = own
    stats[...] = jnp.concatenate(totals + corrections, axis=0)


def spread(bias):
    rows = [jnp.broadcast_to(bias[j : j + 1], (PAGE, TOK)) for j in range(PG)]
    return jnp.concatenate(rows, axis=0)


def key_kernel(
    first, count, flags, k, v, own_dk, own_dv, near, near_stats, far, wrapped, far_stats, bias, *rest
):
    dk_out, dv_out, held, sems = rest[-4:]
    k, v = load((k, v), first, count, held, sems)
    biases = bias[...]
    for h in range(count):
        cols, second = slice(h * D, (h + 1) * D), slice((count + h) * D, (count + h + 1) * D)
        keys, values = k[:, cols], v[:, cols]
        grad_k, grad_v = own_dk[:, cols], own_dv[:, cols]
        if wrapped is None:
            far_pair = (far[:, cols], far[:, second])
        else:
            use = flags[1] > 0
            far_pair = (pick(use, far, wrapped, cols), pick(use, far, wrapped, second))
        pairs = ((near[:, cols], near[:, second]), far_pair)
        for src, ((queries, cotangent), stats) in enumerate(zip(pairs, (near_stats, far_stats))):
            total, correction = stats[h : h + 1], stats[count + h : count + h + 1]
            masks = spread(biases[9 + 3 * src : 12 + 3 * src])
            prob = jnp.exp2(dot(keys, queries, NT) * SCALE2 + masks - total)
            dscore = prob * (dot(values, cotangent, NT) - correction)
            grad_v = grad_v + dot(prob.astype(jnp.bfloat16), cotangent, NN)
            grad_k = grad_k + dot(dscore.astype(jnp.bfloat16), queries, NN)
        dk_out[:, cols] = (grad_k * SCALE).astype(dk_out.dtype)
        dv_out[:, cols] = grad_v.astype(dv_out.dtype)


def block(count, first):
    return pl.BlockSpec((TOK, count * D), lambda i: (0, first // count))


def whole(array):
    return pl.BlockSpec(array.shape, lambda i: (0, 0))


HBM = pl.BlockSpec(memory_space=pltpu.HBM)


def pack_kernel(first, count, k, v, q, do, key_value, query_cot, sems):
    cols = pl.ds(first * D, count * D)
    copies = []
    for n, (array, out, at) in enumerate(
        ((k, key_value, 0), (v, key_value, 1), (q, query_cot, 0), (do, query_cot, 1))
    ):
        to = out.at[:, pl.ds(at * count * D, count * D)]
        copies.append(pltpu.make_async_copy(array.at[:, cols], to, sems.at[n]))
    for copy in copies:
        copy.start()
    for copy in copies:
        copy.wait()


def pack(first, count, *arrays):
    shape = jax.ShapeDtypeStruct((TOK, 2 * count * D), jnp.bfloat16)
    return pl.pallas_call(
        functools.partial(pack_kernel, first, count),
        name="pack",
        in_specs=[HBM] * 4,
        out_specs=[pl.BlockSpec(memory_space=pltpu.VMEM)] * 2,
        out_shape=[shape, shape],
        scratch_shapes=[pltpu.SemaphoreType.DMA((4,))],
        cost_estimate=pl.CostEstimate(
            flops=0, bytes_accessed=16 * TOK * count * D, transcendentals=0
        ),
    )(*arrays)


def call(kernel, name, first, count, flags, ins, loaded, outs, carried, dots, pairs):
    held = [pair for pair in ins if pair is not None]
    present = [pair is not None for pair in ins]
    arrays = [flags] + [a for a, _ in held]
    in_specs = [pl.BlockSpec(memory_space=pltpu.SMEM)] + [s for _, s in held]
    aliases = {}
    for at, array in enumerate(carried):
        aliases[len(arrays)] = at
        arrays.append(array)
        in_specs.append(pl.BlockSpec(memory_space=pl.ANY))

    def run(flags_ref, *refs):
        refs = list(refs)
        given = [refs.pop(0) if here else None for here in present]
        kernel(first, count, flags_ref, *given, *refs)

    return pl.pallas_call(
        run,
        name=name,
        grid=(1,),
        in_specs=in_specs,
        out_specs=[s for _, s in outs],
        out_shape=[s for s, _ in outs],
        input_output_aliases=aliases,
        scratch_shapes=[
            pltpu.VMEM((loaded, TOK, count * D), jnp.bfloat16),
            pltpu.SemaphoreType.DMA((loaded,)),
        ],
        compiler_params=pltpu.CompilerParams(
            dimension_semantics=("arbitrary",), vmem_limit_bytes=48 * 1024 * 1024
        ),
        cost_estimate=pl.CostEstimate(
            flops=2 * dots * count * TOK * TOK * D,
            bytes_accessed=len(held) * count * TOK * D * 2,
            transcendentals=pairs * count * TOK * TOK,
        ),
    )(*arrays)


def biases_of(page_mask, block_at, block_count):
    def picked(at, source):
        part = lax.dynamic_slice(
            page_mask, (jnp.minimum(at, block_count - 1) * PG, source, 0), (PG, 1, PG)
        )[:, 0, :]
        return jnp.where(at < block_count, part, 0)

    parts = [picked(block_at, source) for source in range(3)]
    parts += [picked(block_at + 1, 1), picked(block_at + lax.axis_size("outer"), 2)]
    wide = jnp.concatenate([jnp.repeat(part, PAGE, axis=0) for part in parts], axis=1)
    wide = jnp.where(wide > 0, 0.0, MASKED).astype(jnp.float32)
    return jnp.concatenate((wide, wide[:, :1]), axis=1).T


def body(queries, key_rows, value_rows, cotangent, page_mask):
    n_inner, n_outer = lax.axis_size("inner"), lax.axis_size("outer")
    inner_at, outer_at = lax.axis_index("inner"), lax.axis_index("outer")
    block_at = inner_at * n_outer + outer_at
    span = n_inner // 2

    def at(i, o):
        return i * n_outer + o

    def back(pairs):
        return [(b, a) for a, b in pairs]

    spots = [(i, o) for i in range(n_inner) for o in range(n_outer)]
    near = [
        (at(i, o), at(i, o + 1) if o + 1 < n_outer else at((i + span) % n_inner, 0)) for i, o in spots
    ]
    ring = [(at(i, o), at(i // span * span + (i + 1) % span, o)) for i, o in spots]
    chain = [(at(i, o), at(i + 1, o)) for i, o in spots if i + 1 < n_inner]
    loop = [(at(i, o), at((i + 1) % n_inner, o)) for i, o in spots]
    hop = [(at(0, o), at(span, o)) for o in range(n_outer)]
    hop += [(at(n_inner - 1, o), at(span - 1, o)) for o in range(n_outer)]

    def send(array, pairs):
        return lax.ppermute(array, AXES, pairs)

    def after(array, *earlier):
        return lax.optimization_barrier((array,) + earlier)[0]

    local = (key_rows, value_rows, queries, cotangent)
    bias = biases_of(page_mask, block_at, n_inner * n_outer)
    flags = jnp.stack((inner_at == span, inner_at == span - 1)).astype(jnp.int32)
    kv0, qc0 = pack(*GROUPS[0], *local)
    near_kv0, near_qc0 = send(kv0, near), send(qc0, back(near))
    far_kv0, far_qc0 = send(kv0, chain), send(qc0, back(chain))
    kv1, qc1 = pack(*GROUPS[1], *local)
    near_kv1 = send(kv1, near)
    far_kv1, far_qc1 = send(kv1, ring), send(qc1, back(ring))
    wrapped = send(jnp.where(inner_at == 0, far_kv1, far_qc1), hop)
    near_qc1 = send(qc1, back(near))
    moved = [
        (near_kv0, near_qc0, far_kv0, far_qc0, None),
        (near_kv1, near_qc1, far_kv1, far_qc1, wrapped),
    ]

    out = jax.ShapeDtypeStruct((TOK, HEADS * D), jnp.bfloat16)
    grad_q, grad_k, grad_v = None, None, None
    for (first, count), (near_kv, near_qc, far_kv, far_qc, wrapped) in zip(GROUPS, moved):
        local = block(count, first)
        stats = jax.ShapeDtypeStruct((2 * count, TOK), jnp.float32)
        part = jax.ShapeDtypeStruct((TOK, count * D), jnp.float32)
        grad_q, stats, own_dk, own_dv = call(
            query_kernel, "query_side", first, count, flags,
            [
                (queries, HBM),
                (cotangent, HBM),
                (key_rows, HBM),
                (value_rows, HBM),
                (near_kv, whole(near_kv)),
                (far_kv, whole(far_kv)),
                None if wrapped is None else (wrapped, whole(wrapped)),
                (bias, whole(bias)),
            ],
            4,
            [(out, local), (stats, whole(stats)), (part, whole(part)), (part, whole(part))],
            [] if grad_q is None else [grad_q], 11, 3,
        )
        near_stats, far_stats = send(stats, back(near)), send(stats, back(loop))
        grad_k, grad_v = call(
            key_kernel, "key_side", first, count, flags,
            [
                (key_rows, HBM),
                (value_rows, HBM),
                (own_dk, whole(own_dk)),
                (own_dv, whole(own_dv)),
                (near_qc, whole(near_qc)),
                (near_stats, whole(near_stats)),
                (far_qc, whole(far_qc)),
                None if wrapped is None else (wrapped, whole(wrapped)),
                (far_stats, whole(far_stats)),
                (bias, whole(bias)),
            ],
            2,
            [(out, local), (out, local)],
            [] if grad_k is None else [grad_k, grad_v], 8, 2,
        )
    return (grad_q, grad_k, grad_v)


def solution(mesh):
    split = P(AXES, None)
    return jax.shard_map(
        body, mesh=mesh, in_specs=(split, split, split, split, P()),
        out_specs=(split, split, split), check_vma=False,
    )
```

```python
import functools
import math

import jax
import jax.numpy as jnp
from jax import lax
from jax.experimental import pallas as pl
from jax.experimental.pallas import tpu as pltpu
from jax.sharding import PartitionSpec as P

HEADS = 8
ROW = 4
D = 128
PAGE = 128
PG = 3
TOK = PG * PAGE
AXES = ("inner", "outer")
MASKED = -1e30
SCALE = 1.0 / math.sqrt(D)
SCALE2 = SCALE * math.log2(math.e)
GROUPS = ((0, 4), (4, 4))
NT = (((1,), (1,)), ((), ()))
NN = (((1,), (0,)), ((), ()))
TN = (((0,), (0,)), ((), ()))


def dot(a, b, dims):
    return lax.dot_general(a, b, dims, preferred_element_type=jnp.float32)


def query_head(queries, cotangent, sources, masks):
    key_at = lax.broadcasted_iota(jnp.int32, (PAGE, PAGE), 0)
    causal = key_at <= lax.broadcasted_iota(jnp.int32, (PAGE, PAGE), 1)
    pages, tops, masses, moments = [], [], [], []
    for src, (keys, values) in enumerate(sources):
        scores, pushes = dot(keys, queries, NT), dot(values, cotangent, NT)
        for j in range(PG):
            lo = j * PAGE if src == 0 else 0
            rows = slice(j * PAGE, (j + 1) * PAGE)
            s, p = scores[rows, lo:], pushes[rows, lo:]
            if src == 0:
                diagonal = jnp.where(causal, s[:, :PAGE], MASKED)
                s = diagonal if j == PG - 1 else jnp.concatenate((diagonal, s[:, PAGE:]), axis=1)
            top = jnp.max(s, axis=0, keepdims=True)
            e = jnp.exp2((s - top) * SCALE2)
            mass = jnp.sum(e, axis=0, keepdims=True)
            moment = jnp.sum(e * p, axis=0, keepdims=True)
            top = top * SCALE2 + masks[3 * src + j][:, lo:]
            if lo:
                zeros = jnp.zeros((1, lo), jnp.float32)
                top = jnp.concatenate((zeros + MASKED, top), axis=1)
                mass = jnp.concatenate((zeros, mass), axis=1)
                moment = jnp.concatenate((zeros, moment), axis=1)
            pages.append((e, p))
            tops.append(top)
            masses.append(mass)
            moments.append(moment)
    highest = functools.reduce(jnp.maximum, tops)
    factors = [jnp.exp2(top - highest) for top in tops]
    mass = functools.reduce(jnp.add, [f * m for f, m in zip(factors, masses)])
    moment = functools.reduce(jnp.add, [f * m for f, m in zip(factors, moments)])
    scale = 1.0 / mass
    correction = moment * scale
    grad_q = 0.0
    own = None
    for src, (keys, values) in enumerate(sources):
        probs, dscores = [], []
        for j in range(PG):
            lo = j * PAGE if src == 0 else 0
            e, p = pages[3 * src + j]
            prob = e * (factors[3 * src + j] * scale)[:, lo:]
            dscore = (prob * (p - correction[:, lo:])).astype(jnp.bfloat16)
            prob = prob.astype(jnp.bfloat16)
            if lo:
                zeros = jnp.zeros((PAGE, lo), jnp.bfloat16)
                dscore = jnp.concatenate((zeros, dscore), axis=1)
                prob = jnp.concatenate((zeros, prob), axis=1)
            dscores.append(dscore)
            probs.append(prob)
        dscore = jnp.concatenate(dscores, axis=0)
        if src == 0:
            own = (dot(dscore, queries, NN), dot(jnp.concatenate(probs, axis=0), cotangent, NN))
        grad_q = grad_q + dot(keys, dscore, TN)
    return highest + jnp.log2(mass), correction, (grad_q * SCALE).T, own


def split(count, h):
    return slice(h * D, (h + 1) * D), slice((count + h) * D, (count + h + 1) * D)


def pair_of(use, usual, other, count, h):
    if other is None:
        return tuple(usual[:, at] for at in split(count, h))
    return tuple(jnp.where(use, other[:, at], usual[:, at]) for at in split(count, h))


def masks_of(flags, first):
    rows = []
    for j in range(PG):
        tiles = [
            jnp.full((1, PAGE), jnp.where(flags[first + i * PG + j] > 0, 0.0, MASKED), jnp.float32)
            for i in range(PG)
        ]
        rows.append(jnp.concatenate(tiles, axis=1))
    return rows


def query_kernel(first, count, flags, qc, kv, near, far, wrapped, *rest):
    last = first + count == HEADS
    if last:
        *earlier, stats, dk_out, dv_out, dq_whole, held, sem = rest
        dq_out = held
    else:
        stats, dk_out, dv_out, dq_out = rest
    at = first * D if last else 0
    masks = masks_of(flags, 2) + masks_of(flags, 11) + masks_of(flags, 20)
    totals, corrections = [], []
    for h in range(count):
        cols, second = split(count, h)
        sources = (
            (kv[:, cols], kv[:, second]),
            (near[:, cols], near[:, second]),
            pair_of(flags[0] > 0, far, wrapped, count, h),
        )
        total, correction, grad_q, own = query_head(qc[:, cols], qc[:, second], sources, masks)
        totals.append(total)
        corrections.append(correction)
        dq_out[:, at + h * D : at + (h + 1) * D] = grad_q.astype(dq_out.dtype)
        dk_out[:, cols], dv_out[:, cols] = own
    stats[...] = jnp.concatenate(totals + corrections, axis=0)
    if last:
        done = 0
        for part in earlier:
            held[:, done : done + part.shape[1]] = part[...]
            done += part.shape[1]
        copy = pltpu.make_async_copy(held, dq_whole, sem)
        copy.start()
        copy.wait()


def spread(rows):
    return jnp.concatenate([jnp.broadcast_to(row, (PAGE, TOK)) for row in rows], axis=0)


def key_head(keys, values, queries, cotangent, stats, count, h, mask):
    total, correction = stats[h : h + 1], stats[count + h : count + h + 1]
    prob = jnp.exp2(dot(keys, queries, NT) * SCALE2 + mask - total)
    dscore = prob * (dot(values, cotangent, NT) - correction)
    return (
        dot(dscore.astype(jnp.bfloat16), queries, NN), dot(prob.astype(jnp.bfloat16), cotangent, NN)
    )


def near_key_kernel(groups, flags, *refs):
    *refs, dk_out, dv_out = refs
    mask = spread(masks_of(flags, 29))
    for at, (first, count) in enumerate(groups):
        kv, own_dk, own_dv, near, stats = refs[5 * at : 5 * at + 5]
        for h in range(count):
            cols, second = split(count, h)
            grad_k, grad_v = key_head(
                kv[:, cols], kv[:, second], near[:, cols], near[:, second], stats, count, h, mask
            )
            to = slice((first + h) * D, (first + h + 1) * D)
            dk_out[:, to] = own_dk[:, cols] + grad_k
            dv_out[:, to] = own_dv[:, cols] + grad_v


def far_key_kernel(groups, flags, dk, dv, *rest):
    *refs, dk_whole, dv_whole, held, sems = rest
    mask = spread(masks_of(flags, 38))
    for at, (first, count) in enumerate(groups):
        kv, far, wrapped, stats = refs[4 * at : 4 * at + 4]
        for h in range(count):
            cols, second = split(count, h)
            grad_k, grad_v = key_head(
                kv[:, cols], kv[:, second], *pair_of(flags[1] > 0, far, wrapped, count, h),
                stats, count, h, mask,
            )
            to = slice((first + h) * D, (first + h + 1) * D)
            held[0, :, to] = ((dk[:, to] + grad_k) * SCALE).astype(held.dtype)
            held[1, :, to] = (dv[:, to] + grad_v).astype(held.dtype)
    copies = [
        pltpu.make_async_copy(held.at[n], whole, sems.at[n])
        for n, whole in enumerate((dk_whole, dv_whole))
    ]
    for copy in copies:
        copy.start()
    for copy in copies:
        copy.wait()


HBM = pl.BlockSpec(memory_space=pltpu.HBM)
VMEM = pl.BlockSpec(memory_space=pltpu.VMEM)


def pack(first, count, left, right):
    cols = slice(first * D, (first + count) * D)
    return jnp.concatenate((left[:, cols], right[:, cols]), axis=1)


def call(kernel, name, count, flags, ins, outs, scratch, dots, pairs):
    present = [array is not None for array in ins]
    arrays = [flags] + [array for array in ins if array is not None]

    def run(flags_ref, *refs):
        refs = list(refs)
        given = [refs.pop(0) if here else None for here in present]
        kernel(flags_ref, *given, *refs)

    return pl.pallas_call(
        run,
        name=name,
        in_specs=[pl.BlockSpec(memory_space=pltpu.SMEM)] + [VMEM] * (len(arrays) - 1),
        out_specs=[
            HBM if shape == jax.ShapeDtypeStruct((TOK, HEADS * D), jnp.bfloat16) else VMEM
            for shape in outs
        ],
        out_shape=outs,
        scratch_shapes=scratch,
        compiler_params=pltpu.CompilerParams(vmem_limit_bytes=40 * 1024 * 1024),
        cost_estimate=pl.CostEstimate(
            flops=2 * dots * count * TOK * TOK * D,
            bytes_accessed=len(ins) * count * TOK * D * 2,
            transcendentals=pairs * count * TOK * TOK,
        ),
    )(*arrays)


def flags_of(page_mask, wraps, block_at, block_count):
    def picked(at, source):
        part = lax.dynamic_slice(
            page_mask, (jnp.minimum(at, block_count - 1) * PG, source, 0), (PG, 1, PG)
        )
        return jnp.where(at < block_count, part, 0).reshape(PG * PG)

    parts = [picked(block_at, source) for source in range(3)]
    parts += [picked(block_at + 1, 1), picked(block_at + lax.axis_size("outer"), 2)]
    return jnp.concatenate([jnp.stack(wraps).astype(jnp.int32)] + parts)


def body(queries, key_rows, value_rows, cotangent, page_mask):
    n_inner, n_outer = lax.axis_size("inner"), lax.axis_size("outer")
    inner_at, outer_at = lax.axis_index("inner"), lax.axis_index("outer")
    block_at = inner_at * n_outer + outer_at
    span = n_inner // 2

    def at(i, o):
        return i * n_outer + o

    def back(pairs):
        return [(b, a) for a, b in pairs]

    spots = [(i, o) for i in range(n_inner) for o in range(n_outer)]
    near = [(at(i, o), at(i, o + 1)) for i, o in spots if o + 1 < n_outer]
    circle = [(at(i, o), at(i, (o + 1) % n_outer)) for i, o in spots]
    ring = [(at(i, o), at(i // span * span + (i + 1) % span, o)) for i, o in spots]
    loop = [(at(i, o), at((i + 1) % n_inner, o)) for i, o in spots]
    swap = [(at(span - 1, o), at(span, o)) for o in range(n_outer)]
    swap += back(swap)

    heights = 2 * n_outer // ROW

    def spot(end, z, y):
        z = z % heights
        half, low = z // (heights // 2), z % (heights // 2)
        return at(half * span + (span - 1 if end else 0), low * ROW + y)

    first_ring, first_back = ring[:], back(ring)
    for z in range(heights):
        old, new = (spot(1, z, ROW - 1), spot(0, z, ROW - 1)), spot(0, z - 1, ROW - 1)
        first_ring[first_ring.index(old)] = (old[0], new)
        old, new = (spot(0, z, ROW - 1), spot(1, z, ROW - 1)), spot(1, z - 1, ROW - 1)
        first_back[first_back.index(old)] = (old[0], new)
    hop = []
    for z in range(heights):
        upper = z >= heights // 2
        for y in range(ROW):
            relay = spot(upper, z - 1 if y == ROW - 1 else z, y)
            hop.append((relay, spot(upper, z - heights // 2, y)))

    def send(array, pairs):
        return lax.ppermute(array, AXES, pairs)

    def after(arrays):
        return lax.optimization_barrier(arrays)

    flags = flags_of(
        page_mask,
        (
            inner_at == span,
            inner_at == span - 1,
        ),
        block_at, n_inner * n_outer,
    )
    kv = [pack(*group, key_rows, value_rows) for group in GROUPS]
    qc = [pack(*group, queries, cotangent) for group in GROUPS]
    near0 = [send(kv[0], near), send(qc[0], back(near))]
    joint1 = [send(jnp.where(inner_at == span - 1, kv[1], qc[1]), swap)]
    far0 = [send(kv[0], first_ring), send(qc[0], first_back)]
    near1 = [send(kv[1], near)]
    joint0 = [send(jnp.where(inner_at % span == 0, far0[0], far0[1]), hop)]
    sides, far0 = after(((kv, qc), far0))
    far1 = [send(sides[0][1], ring), send(sides[1][1], back(ring))]
    later, near0 = after((qc[1], near0))
    near1.append(send(later, back(near)))
    near_kv, near_qc, far_kv, far_qc, wrapped = zip(near0 + far0 + joint0, near1 + far1 + joint1)

    grad_q, own, all_stats = [], [], []
    for turn, (first, count) in enumerate(GROUPS):
        last = first + count == HEADS
        stats = jax.ShapeDtypeStruct((2 * count, TOK), jnp.float32)
        part = jax.ShapeDtypeStruct((TOK, count * D), jnp.float32)
        out = jax.ShapeDtypeStruct((TOK, (HEADS if last else count) * D), jnp.bfloat16)
        held = [pltpu.VMEM(out.shape, out.dtype), pltpu.SemaphoreType.DMA] if last else []
        stats, own_dk, own_dv, grad = call(
            functools.partial(query_kernel, first, count), "query_side", count, flags,
            [qc[turn], kv[turn], near_kv[turn], far_kv[turn], wrapped[turn], *grad_q],
            [stats, part, part, out], held, 11, 3,
        )
        grad_q.append(grad)
        own.append((own_dk, own_dv))
        all_stats.append(stats)
    stats = jnp.concatenate(all_stats, axis=0)
    far_stats, near_stats = send(stats, back(loop)), send(stats, back(circle))
    ends = [2 * (first + count) for first, count in GROUPS]
    near_ins, far_ins = [], []
    for turn, (_, count) in enumerate(GROUPS):
        rows = slice(ends[turn] - 2 * count, ends[turn])
        near_ins += [kv[turn], *own[turn], near_qc[turn], near_stats[rows]]
        far_ins += [kv[turn], far_qc[turn], wrapped[turn], far_stats[rows]]
    sums = jax.ShapeDtypeStruct((TOK, HEADS * D), jnp.float32)
    dk, dv = call(
        functools.partial(near_key_kernel, GROUPS), "near_keys", HEADS, flags, near_ins,
        [sums, sums], [], 4, 1,
    )
    out = jax.ShapeDtypeStruct((TOK, HEADS * D), jnp.bfloat16)
    grad_k, grad_v = call(
        functools.partial(far_key_kernel, GROUPS), "far_keys", HEADS, flags, [dk, dv, *far_ins],
        [out, out],
        [pltpu.VMEM((2, *out.shape), out.dtype), pltpu.SemaphoreType.DMA((2,))], 4, 1,
    )
    return (grad_q[-1], grad_k, grad_v)


def solution(mesh):
    split = P(AXES, None)
    return jax.shard_map(
        body, mesh=mesh, in_specs=(split, split, split, split, P()),
        out_specs=(split, split, split), check_vma=False,
    )
```
